32 devices in a mesh: row: 4 (over y, core), col: 4 (over z), seq: 2 (over x).
Axes of the slice: x: 2, y: 2, z: 4, core: 2. Of those that a mesh axis runs over, the one named last changes fastest.
Arguments:
- queries: bfloat16 [4, 2048, 8192], P('row', 'seq', 'col'), may hold values from -120 to 120
- rotated_key_heads: bfloat16 [4, 2048, 1024], P('row', 'seq', 'col'), may hold values from -7 to 7
- value_head_states: bfloat16 [4, 2048, 1024], P('row', 'seq', 'col'), may hold values from -6 to 6
- document_index: int32 [4, 2048], P('row'), may hold values from 0 to 3, never falling along the last dimension, each value on 1 to 1024 neighbouring positions
- output_projection_weight: bfloat16 [8192, 8192], P('col', 'row'), may hold values from -0.1875 to 0.1875
- frozen_down_factor: bfloat16 [8192, 256], P('col'), may hold values from -0.1875 to 0.1875
- trained_up_factor: bfloat16 [256, 8192], P(None, 'row'), may hold values from -0.125 to 0.125
- correction_tiles: bfloat16 [4, 4, 5, 128, 128], P('row', 'col'), may hold values from -1.1953125 to 1.1953125
- tile_placement: int32 [4, 4, 5, 2], P('row', 'col'), may hold values from 0 to 15, as said below
- cotangent: bfloat16 [4, 2048, 8192], P(None, 'seq', ('row', 'col')), may hold values from -0.06591797 to 0.06591797
Outputs:
- projected: bfloat16 [4, 2048, 8192], P(None, 'seq', ('row', 'col'))
- up_factor_gradient: float32 [256, 8192], P(None, 'row')
- grad_tiles: float32 [4, 4, 5, 128, 128], P('row', 'col')
The draws below stay inside these ranges and needn't reach their ends.
Inputs may be any that keep to these rules, and one draw needn't show every extreme that they name: `tile_placement`: inside one block of the weight grid the 5 tiles are different; entry 0 is a tile row below 16, entry 1 a tile column below 16.
All inputs are finite; a program needn't handle non-finite values.
Results may differ from the reference program's by a relative error of at most 0.0054.
Values may be sent and summed in bfloat16 or wider, within the bound.
No kernel may reach another device: no remote copies, remote signals or barrier semaphores. Data moves between devices by JAX's collectives and lax.ppermute only.
A program may use at most 192 MiB of HBM per device.

```python
import math
import jax
import jax.numpy as jnp
import numpy as np
from jax import lax

MODEL_WIDTH = 8192
QUERY_HEADS = 64
KEY_VALUE_HEADS = 8
HEAD_WIDTH = 128
CORRECTION_RANK = 256
TILE = 128
SEQUENCE_LENGTH = 2048
SEQUENCE_COUNT = 4
DTB = 5
N_ROW = 4
N_COL = 4


def query_key_pair(key):
    random_key_query = jax.random.fold_in(key, 101)
    random_key_for_keys = jax.random.fold_in(key, 102)
    query_group_width = QUERY_HEADS // KEY_VALUE_HEADS
    random_key_draw = jnp.clip(jax.random.normal(random_key_for_keys, (SEQUENCE_COUNT, SEQUENCE_LENGTH, KEY_VALUE_HEADS, HEAD_WIDTH), jnp.float32), -5.0, 5.0)
    random_query_draw = jnp.clip(2.0 * jax.random.normal(random_key_query, (SEQUENCE_COUNT, SEQUENCE_LENGTH, KEY_VALUE_HEADS, query_group_width, HEAD_WIDTH), jnp.float32), -12.0, 12.0)
    return (random_query_draw.reshape(SEQUENCE_COUNT, SEQUENCE_LENGTH, QUERY_HEADS * HEAD_WIDTH), random_key_draw.reshape(SEQUENCE_COUNT, SEQUENCE_LENGTH, KEY_VALUE_HEADS * HEAD_WIDTH))


def draw_queries(key, part):
    return query_key_pair(key)[0].astype(jnp.bfloat16)


def draw_rotated_key_heads(key, part):
    return query_key_pair(key)[1].astype(jnp.bfloat16)


def to_front(order, wanted):
    position = jnp.argmax((order == wanted).astype(jnp.int32))
    first = order[0]
    return order.at[position].set(first).at[0].set(wanted)


def draw_tile_placement(key, part):
    in_tiles = QUERY_HEADS * HEAD_WIDTH // N_COL // TILE
    out_tiles = MODEL_WIDTH // N_ROW // TILE
    total = in_tiles * out_tiles
    block_keys = jax.random.split(jax.random.fold_in(key, 303), N_ROW * N_COL)
    orders = jax.vmap(lambda single: jax.random.permutation(single, total))(block_keys).astype(jnp.int32)
    orders = orders.at[0].set(to_front(orders[0], total - 1))
    last_block = N_ROW * N_COL - 1
    orders = orders.at[last_block].set(to_front(orders[last_block], 0))
    chosen = orders[:, :DTB].reshape(N_ROW, N_COL, DTB)
    return jnp.stack([chosen // out_tiles, chosen % out_tiles], axis=-1).astype(jnp.int32)


def level_of(key, extent, cuts, least, high):
    def one(dim, blocks):
        heights = jax.random.uniform(jax.random.fold_in(jax.random.fold_in(key, 6), dim), (blocks,), jnp.float32, least / len(cuts), high / len(cuts))
        return jnp.repeat(jnp.exp(heights), extent[dim] // blocks).reshape((-1,) + (1,) * (len(extent) - dim - 1))

    gain = one(*cuts[0])
    for cut in cuts[1:]:
        gain = gain * one(*cut)
    return gain


def split_up(amount, total, most, lean):
    weights = [(1 << 20) // math.isqrt(standing ** lean) + 1 for standing in range(2, amount + 1)]
    rest, holding = total - most - (amount - 1), [1] * (amount - 1)
    while rest > 0:
        free = [i for i in range(amount - 1) if holding[i] < most]
        mass, remaining = sum([weights[i] for i in free]), rest
        for i in free:
            addition = min(most - holding[i], max(1, remaining * weights[i] // mass), rest)
            holding[i] = holding[i] + addition
            rest = rest - addition
    return np.array([most] + holding)


def uneven_parts(own_key, number_of, total, most, lean):
    if number_of == 2:
        one = jax.random.randint(own_key, (), max(1, total - most), min(most, total - 1) + 1)
        return jnp.stack([one, total - one])
    sizes = jnp.asarray(split_up(number_of, total, most, lean), jnp.int32)
    pairs = (number_of - 1) // 2
    donor, sink = sizes[1:1 + 2 * pairs:2], sizes[2:2 + 2 * pairs:2]
    margin = jnp.minimum(donor - 1, most - sink)
    moved = jax.random.randint(jax.random.fold_in(own_key, 1), (pairs,), 0, 1 << 20) % (margin + 1)
    sizes = sizes.at[1:1 + 2 * pairs:2].set(donor - moved).at[2:2 + 2 * pairs:2].set(sink + moved)
    return sizes[jax.random.permutation(jax.random.fold_in(own_key, 2), number_of)]


def bell_draw(stream_key, dims, scale, most, cuts=(), kind=jnp.bfloat16):
    result = scale * jax.random.normal(stream_key, dims, jnp.float32)
    if cuts:
        result = result * level_of(stream_key, dims, cuts, -0.22, 0.18)
    return jnp.clip(result, -most, most).astype(kind)


def setup_inputs(seed: int = 0) -> dict:
    keys = jax.random.split(jax.random.key(seed), 11)
    queries = draw_queries(jax.random.fold_in(keys[10], 71), 0)
    rotated_key_heads = draw_rotated_key_heads(jax.random.fold_in(keys[10], 71), 0)
    value_head_states = bell_draw(keys[2], (SEQUENCE_COUNT, SEQUENCE_LENGTH, KEY_VALUE_HEADS * HEAD_WIDTH), 1.0, 6.0, ((0, 4), (1, 2), (2, 4)))
    document_index = jax.vmap(lambda own: jnp.searchsorted(jnp.cumsum(uneven_parts(own, 4, SEQUENCE_LENGTH, SEQUENCE_LENGTH // 2, 0)), jnp.arange(SEQUENCE_LENGTH), side="right"))(jax.random.split(keys[3], SEQUENCE_COUNT)).reshape((SEQUENCE_COUNT, SEQUENCE_LENGTH)).astype(jnp.int32)
    output_projection_weight = bell_draw(keys[4], (QUERY_HEADS * HEAD_WIDTH, MODEL_WIDTH), (QUERY_HEADS * HEAD_WIDTH // 8) ** -0.5, 0.1875, ((0, 4), (1, 4)))
    frozen_down_factor = bell_draw(keys[5], (QUERY_HEADS * HEAD_WIDTH, CORRECTION_RANK), (QUERY_HEADS * HEAD_WIDTH // 8) ** -0.5, 0.1875, ((0, 4),))
    trained_up_factor = bell_draw(keys[6], (CORRECTION_RANK, MODEL_WIDTH), (8 * CORRECTION_RANK) ** -0.5, 0.125, ((1, 4),))
    correction_tiles = bell_draw(keys[7], (N_ROW, N_COL, DTB, TILE, TILE), 0.2, 1.1953125, ((0, 4), (1, 4)))
    tile_placement = draw_tile_placement(jax.random.fold_in(keys[10], 71), 0)
    cotangent = bell_draw(keys[9], (SEQUENCE_COUNT, SEQUENCE_LENGTH, MODEL_WIDTH), ((SEQUENCE_COUNT * SEQUENCE_LENGTH) ** -0.5), 0.06591797, ((1, 2), (2, 16)))
    return {"queries": queries, "rotated_key_heads": rotated_key_heads, "value_head_states": value_head_states, "document_index": document_index, "output_projection_weight": output_projection_weight, "frozen_down_factor": frozen_down_factor, "trained_up_factor": trained_up_factor, "correction_tiles": correction_tiles, "tile_placement": tile_placement, "cotangent": cotangent}


low_rank_factor = 2.0


def one_head(operands):
    query_h, key_h, value_h, documents = operands
    score_scale = HEAD_WIDTH ** -0.5
    positions = jnp.arange(SEQUENCE_LENGTH, dtype=jnp.int32)
    causal = positions[None, :] <= positions[:, None]
    scores = jnp.einsum("qgd,sd->gqs", query_h.astype(jnp.float32), key_h.astype(jnp.float32), precision=lax.Precision.HIGHEST) * score_scale
    visible = (causal & (documents[None, :] == documents[:, None]))[None]
    row_max = jnp.max(jnp.where(visible, scores, -jnp.inf), axis=-1, keepdims=True)
    weights = jnp.exp(jnp.where(visible, scores - row_max, -jnp.inf))
    row_total = jnp.sum(weights, axis=-1)
    rounded = lax.optimization_barrier(weights.astype(jnp.bfloat16))
    mixed_rows = jnp.einsum("gqs,sd->qgd", rounded.astype(jnp.float32), value_h.astype(jnp.float32), precision=lax.Precision.HIGHEST)
    return (mixed_rows / row_total.T[:, :, None]).astype(jnp.bfloat16)


def reference(queries, rotated_key_heads, value_head_states, document_index, output_projection_weight, frozen_down_factor, trained_up_factor, correction_tiles, tile_placement, cotangent):
    query_group_width = QUERY_HEADS // KEY_VALUE_HEADS
    sequence_rows = queries.shape[0]
    query_head_matrix = queries.reshape(sequence_rows, SEQUENCE_LENGTH, KEY_VALUE_HEADS, query_group_width, HEAD_WIDTH).transpose(0, 2, 1, 3, 4).reshape(sequence_rows * KEY_VALUE_HEADS, SEQUENCE_LENGTH, query_group_width, HEAD_WIDTH)
    key_head_matrix = rotated_key_heads.reshape(sequence_rows, SEQUENCE_LENGTH, KEY_VALUE_HEADS, HEAD_WIDTH).transpose(0, 2, 1, 3).reshape(sequence_rows * KEY_VALUE_HEADS, SEQUENCE_LENGTH, HEAD_WIDTH)
    value_head_matrix = value_head_states.reshape(sequence_rows, SEQUENCE_LENGTH, KEY_VALUE_HEADS, HEAD_WIDTH).transpose(0, 2, 1, 3).reshape(sequence_rows * KEY_VALUE_HEADS, SEQUENCE_LENGTH, HEAD_WIDTH)
    document_tiled = jnp.repeat(document_index, KEY_VALUE_HEADS, axis=0)
    attention_output = lax.map(one_head, (query_head_matrix, key_head_matrix, value_head_matrix, document_tiled))
    attention_output = attention_output.reshape(sequence_rows, KEY_VALUE_HEADS, SEQUENCE_LENGTH, query_group_width, HEAD_WIDTH).transpose(0, 2, 1, 3, 4).reshape(sequence_rows, SEQUENCE_LENGTH, QUERY_HEADS * HEAD_WIDTH)
    token_count = sequence_rows * SEQUENCE_LENGTH
    flattened_rows = attention_output.reshape(token_count, QUERY_HEADS * HEAD_WIDTH)
    frozen_product = jnp.dot(flattened_rows, output_projection_weight, preferred_element_type=jnp.float32)
    low_rank_inner = jnp.dot(flattened_rows, frozen_down_factor, preferred_element_type=jnp.float32).astype(jnp.bfloat16)
    low_rank_product = jnp.dot(low_rank_inner, trained_up_factor, preferred_element_type=jnp.float32)
    in_block = QUERY_HEADS * HEAD_WIDTH // N_COL
    out_block = MODEL_WIDTH // N_ROW
    row_ids = jnp.arange(N_ROW, dtype=jnp.int32)[:, None, None]
    col_ids = jnp.arange(N_COL, dtype=jnp.int32)[None, :, None]
    in_start = (col_ids * in_block + tile_placement[..., 0] * TILE).reshape(-1).astype(jnp.int32)
    out_start = (row_ids * out_block + tile_placement[..., 1] * TILE).reshape(-1).astype(jnp.int32)
    offsets = jnp.arange(TILE, dtype=jnp.int32)
    in_index = in_start[:, None] + offsets[None, :]
    out_index = out_start[:, None] + offsets[None, :]
    tile_values = correction_tiles.reshape(-1, TILE, TILE).astype(jnp.float32)
    picked = flattened_rows[:, in_index].astype(jnp.float32)
    tile_terms = jnp.einsum("tni,nio->tno", picked, tile_values, precision=lax.Precision.HIGHEST)
    tile_sparse_piece = jnp.zeros((token_count, MODEL_WIDTH), jnp.float32).at[:, out_index].add(tile_terms)
    projected = (frozen_product + low_rank_factor * low_rank_product + tile_sparse_piece).astype(jnp.bfloat16).reshape(sequence_rows, SEQUENCE_LENGTH, MODEL_WIDTH)
    output_gradient_rows = cotangent.reshape(token_count, MODEL_WIDTH)
    up_factor_gradient = low_rank_factor * jnp.dot(low_rank_inner.T, output_gradient_rows, preferred_element_type=jnp.float32)
    cot_picked = output_gradient_rows.astype(jnp.float32)[:, out_index]
    grad_tiles = jnp.einsum("tni,tno->nio", picked, cot_picked, precision=lax.Precision.HIGHEST)
    grad_tiles = grad_tiles.reshape(N_ROW, N_COL, DTB, TILE, TILE)
    return projected, up_factor_gradient, grad_tiles
```

```python
import functools

import jax
import jax.numpy as jnp
from jax import lax
from jax.experimental import pallas as pl
from jax.experimental.pallas import tpu as pltpu
from jax.sharding import PartitionSpec as P

HEAD_WIDTH = 128
TILE = 128
F32 = jnp.float32
BF16 = jnp.bfloat16
LOW_RANK_FACTOR = 2.0
NEG = -1e30
LOG2E = 1.4426950408889634


def attend_kernel(bounds_ref, q_ref, k_ref, vt_ref, start_ref, o_ref, *, heads, key_block, first, blocks):
    rows = q_ref.shape[0]
    block = first + pl.program_id(2)
    scale = HEAD_WIDTH ** (-0.5) * LOG2E
    starts = start_ref[...]
    positions = bounds_ref[2 * blocks] + block * rows + lax.broadcasted_iota(jnp.int32, (1, rows), 1)
    queries = [q_ref[:, h * HEAD_WIDTH:(h + 1) * HEAD_WIDTH] for h in range(heads)]

    def step(at, carry):
        base = pl.multiple_of(at * key_block, key_block)
        keys = k_ref[pl.ds(base, key_block), :]
        values = vt_ref[:, pl.ds(base, key_block)]
        key_pos = base + lax.broadcasted_iota(jnp.int32, (key_block, rows), 0)
        visible = (key_pos >= starts) & (key_pos <= positions)
        out = []
        for h in range(heads):
            top, total, acc = carry[h]
            scores = lax.dot_general(
                keys, queries[h], (((1,), (1,)), ((), ())), preferred_element_type=F32
            )
            scores = jnp.where(visible, scores * scale, NEG)
            new_top = jnp.maximum(top, jnp.max(scores, axis=0, keepdims=True))
            probs = jnp.exp2(scores - new_top)
            fade = jnp.exp2(top - new_top)
            total = total * fade + jnp.sum(probs, axis=0, keepdims=True)
            acc = acc * fade + jnp.dot(values, probs.astype(BF16), preferred_element_type=F32)
            out.append((new_top, total, acc))
        return tuple(out)

    start = tuple(
        (
            jnp.full((1, rows), NEG, F32),
            jnp.zeros((1, rows), F32),
            jnp.zeros((HEAD_WIDTH, rows), F32),
        )
        for _ in range(heads)
    )
    done = lax.fori_loop(bounds_ref[block], bounds_ref[blocks + block], step, start)
    for h in range(heads):
        _, total, acc = done[h]
        o_ref[:, h * HEAD_WIDTH:(h + 1) * HEAD_WIDTH] = jnp.transpose(acc / total).astype(BF16)


def attend_chunk(queries, keys, values_t, bounds, starts, offset, rows, block_rows, key_block):
    length, width = queries.shape
    key_len = keys.shape[0]
    kv_heads = keys.shape[1] // HEAD_WIDTH
    group = width // HEAD_WIDTH // kv_heads
    heads = min(4, group)
    steps = group // heads
    first = offset // block_rows
    grid_spec = pltpu.PrefetchScalarGridSpec(
        num_scalar_prefetch=1,
        grid=(kv_heads, steps, rows // block_rows),
        in_specs=[
            pl.BlockSpec((block_rows, heads * HEAD_WIDTH), lambda g, s, i, b: (first + i, g * steps + s)),
            pl.BlockSpec((key_len, HEAD_WIDTH), lambda g, s, i, b: (0, g)),
            pl.BlockSpec((HEAD_WIDTH, key_len), lambda g, s, i, b: (g, 0)),
            pl.BlockSpec((1, block_rows), lambda g, s, i, b: (0, first + i)),
        ],
        out_specs=pl.BlockSpec((block_rows, heads * HEAD_WIDTH), lambda g, s, i, b: (i, g * steps + s)),
    )
    work = rows * key_len // 3 * width
    return pl.pallas_call(
        functools.partial(
            attend_kernel, heads=heads, key_block=key_block, first=first, blocks=length // block_rows
        ),
        out_shape=jax.ShapeDtypeStruct((rows, width), BF16),
        grid_spec=grid_spec,
        compiler_params=pltpu.CompilerParams(vmem_limit_bytes=32 * 1024 * 1024),
        cost_estimate=pl.CostEstimate(
            flops=8 * work, bytes_accessed=4 * rows * width, transcendentals=work // HEAD_WIDTH
        ),
        name="attention",
    )(bounds, queries, keys, values_t, starts)


def add_tiles_kernel(in_ref, out_tile_ref, w_ref, tiles_ref, o_ref):
    o_ref[...] = w_ref[...]
    for t in range(tiles_ref.shape[0]):

        @pl.when(in_ref[t] == pl.program_id(0))
        def _(t=t):
            at = pl.ds(pl.multiple_of(out_tile_ref[t] * TILE, TILE), TILE)
            o_ref[:, at] = (o_ref[:, at].astype(F32) + tiles_ref[t].astype(F32)).astype(BF16)


def add_tiles(weight, tiles, tile_in, tile_out):
    depth, out_width = weight.shape
    grid_spec = pltpu.PrefetchScalarGridSpec(
        num_scalar_prefetch=2,
        grid=(depth // TILE,),
        in_specs=[
            pl.BlockSpec((TILE, out_width), lambda i, ti, to: (i, 0)),
            pl.BlockSpec(tiles.shape, lambda i, ti, to: (0, 0, 0)),
        ],
        out_specs=pl.BlockSpec((TILE, out_width), lambda i, ti, to: (i, 0)),
    )
    return pl.pallas_call(
        add_tiles_kernel,
        out_shape=jax.ShapeDtypeStruct(weight.shape, BF16),
        grid_spec=grid_spec,
        cost_estimate=pl.CostEstimate(flops=0, bytes_accessed=4 * depth * out_width, transcendentals=0),
        name="add_tiles",
    )(tile_in, tile_out, weight, tiles)


def tile_grad_kernel(in_ref, slot_ref, out_tile_ref, order_ref, *refs):
    o_ref = refs[-1]
    count = (len(refs) - 1) // 2
    total = jnp.zeros(o_ref.shape[1:], F32)
    for j in range(count):
        total += lax.dot_general(
            refs[j][0], refs[count + j][0, 0], (((0,), (0,)), ((), ())), preferred_element_type=F32
        )
    o_ref[0] = total


def tile_grads(halves, cot, tile_in, tile_slot, tile_out, order):
    rows = cot.shape[2]
    tiles = tile_in.shape[0]
    arrays, a_specs, c_specs = [], [], []
    for half in halves:
        for b in range(half.shape[0]):
            j = len(arrays)
            arrays.append(half)
            a_specs.append(pl.BlockSpec((1, rows, TILE), lambda t, ti, ts, to, od, b=b: (b, 0, ti[t])))
            c_specs.append(
                pl.BlockSpec((1, 1, rows, TILE), lambda t, ti, ts, to, od, j=j: (ts[t], od[j], 0, to[t]))
            )
    batches = len(arrays)
    grid_spec = pltpu.PrefetchScalarGridSpec(
        num_scalar_prefetch=4,
        grid=(tiles,),
        in_specs=a_specs + c_specs,
        out_specs=pl.BlockSpec((1, TILE, TILE), lambda t, ti, ts, to, od: (t, 0, 0)),
    )
    return pl.pallas_call(
        tile_grad_kernel,
        out_shape=jax.ShapeDtypeStruct((tiles, TILE, TILE), F32),
        grid_spec=grid_spec,
        compiler_params=pltpu.CompilerParams(vmem_limit_bytes=16 * 1024 * 1024),
        cost_estimate=pl.CostEstimate(
            flops=2 * tiles * batches * rows * TILE * TILE,
            bytes_accessed=4 * tiles * batches * rows * TILE,
            transcendentals=0,
        ),
        name="tile_gradient",
    )(tile_in, tile_slot, tile_out, order, *arrays, *([cot] * batches))


def up_grad_kernel(col_ref, low_ref, cot_ref, sum_ref, o_ref):
    o_ref[...] = sum_ref[...] + LOW_RANK_FACTOR * lax.dot_general(
        low_ref[...], cot_ref[0], (((0,), (0,)), ((), ())), preferred_element_type=F32
    )


def up_grad(col, low, cot, total):
    slots, length, segment = cot.shape
    rank = low.shape[1]
    grid_spec = pltpu.PrefetchScalarGridSpec(
        num_scalar_prefetch=1,
        grid=(slots,),
        in_specs=[
            pl.BlockSpec((length, rank), lambda k, c: (0, 0)),
            pl.BlockSpec((1, length, segment), lambda k, c: (k, 0, 0)),
            pl.BlockSpec((rank, segment), lambda k, c: (0, lax.rem(k + c[0], slots))),
        ],
        out_specs=pl.BlockSpec((rank, segment), lambda k, c: (0, lax.rem(k + c[0], slots))),
    )
    return pl.pallas_call(
        up_grad_kernel,
        out_shape=jax.ShapeDtypeStruct(total.shape, F32),
        grid_spec=grid_spec,
        input_output_aliases={3: 0},
        compiler_params=pltpu.CompilerParams(vmem_limit_bytes=24 * 1024 * 1024),
        cost_estimate=pl.CostEstimate(
            flops=2 * slots * length * segment * rank,
            bytes_accessed=2 * slots * length * segment,
            transcendentals=0,
        ),
        name="up_gradient",
    )(col[None], low, cot, total)


def swap(value, axis, bit, size):
    return lax.ppermute(value, axis, [(i, i ^ bit) for i in range(size)])


def row_bits(size):
    bits = []
    bit = size // 2
    while bit >= 1:
        bits.append(bit)
        bit //= 2
    return bits


def gather_row(value, size):
    pieces, slots = value, [0]
    halves = [pieces]
    for bit in row_bits(size):
        if len(halves) > 1:
            pieces = jnp.concatenate(halves, axis=0)
        halves = [pieces, swap(pieces, "row", bit, size)]
        slots = slots + [s ^ bit for s in slots]
    return halves, slots


def add_over_seq(value, size):
    if size == 2:
        return value + swap(value, "seq", 1, size)
    return lax.psum(value, "seq")


def hop(value, way, size, senders):
    pairs = [(i, i + 1) for i in senders if i + 1 < size]
    if way < 0:
        pairs = [(size - 1 - a, size - 1 - b) for a, b in pairs]
    return lax.ppermute(value, "col", pairs)


def by_slot(from_left, from_right, size):
    me = lax.axis_index("col")
    return [
        jnp.where(me + k < size, from_right[k - 1], from_left[size - 1 - k]) for k in range(1, size)
    ]


def target(way, t, size):
    me = lax.axis_index("col")
    last = size - 1
    return jnp.clip(last - t + me if way > 0 else t + me - last, 0, last)


def chunk_list(length, block):
    if length < 4 * block:
        return [(at, block) for at in range(0, length, block)]
    return [(0, block), (block, block)] + [(at, 2 * block) for at in range(2 * block, length, 2 * block)]


def low_rank_steps(partial, col, n_col, n_row):
    current = partial
    for bit in row_bits(n_col):
        half = current.shape[0] // 2
        upper = jnp.bitwise_and(col, bit) != 0
        keep = jnp.where(upper, current[half:], current[:half])
        give = jnp.where(upper, current[:half], current[half:])
        arrived = yield (lambda v, bit=bit: swap(v, "col", bit, n_col)), give.astype(BF16)
        current = keep + arrived.astype(F32)
    current = current.astype(BF16)
    for bit in reversed(row_bits(n_col)):
        arrived = yield (lambda v, bit=bit: swap(v, "col", bit, n_col)), current
        upper = jnp.bitwise_and(col, bit) != 0
        current = jnp.concatenate(
            [jnp.where(upper, arrived, current), jnp.where(upper, current, arrived)]
        )
    current = current[None]
    for bit in row_bits(n_row):
        arrived = yield (lambda v, bit=bit: swap(v, "row", bit, n_row)), current
        current = jnp.concatenate([current, arrived])
    yield "done", current


def tie(*values):
    return lax.optimization_barrier(values)


def local(
    queries,
    rotated_key_heads,
    value_head_states,
    document_index,
    output_projection_weight,
    frozen_down_factor,
    trained_up_factor,
    correction_tiles,
    tile_placement,
    cotangent,
):
    n_row, n_col, n_seq = lax.axis_size("row"), lax.axis_size("col"), lax.axis_size("seq")
    row, col, seq = lax.axis_index("row"), lax.axis_index("col"), lax.axis_index("seq")
    local_len, width = queries.shape[1], queries.shape[2]
    out_width = output_projection_weight.shape[1]
    segment = out_width // n_col
    seg_tiles = segment // TILE
    rank = frozen_down_factor.shape[1]
    block_rows = max(128, local_len // 4)
    chunks = chunk_list(local_len, block_rows)
    half_rows = n_row // 2
    ways = (1, -1)

    here = jnp.stack([rotated_key_heads[0], value_head_states[0]])
    if n_seq == 2:
        other = swap(here, "seq", 1, 2)
        both = jnp.concatenate([jnp.where(seq == 0, here, other), jnp.where(seq == 0, other, here)], axis=1)
    else:
        both = lax.all_gather(here, "seq", axis=1, tiled=True)
    keys, values_t = both[0], both[1].T
    key_block = min(256, keys.shape[0])
    documents = document_index[0]
    starts_all = jnp.searchsorted(documents, documents, side="left", method="compare_all").astype(jnp.int32)
    base = seq * local_len
    starts = lax.dynamic_slice_in_dim(starts_all, base, local_len, 0)
    block_at = jnp.arange(local_len // block_rows) * block_rows
    bounds = jnp.concatenate(
        [starts[block_at] // key_block, (base + block_at + block_rows - 1) // key_block + 1, base[None]]
    ).astype(jnp.int32)

    first_hop = {way: hop(cotangent, way, n_col, range(n_col)) for way in ways}

    gathered, low_parts = [], []
    for offset, rows in chunks:
        part = attend_chunk(
            queries[0], keys, values_t, bounds, starts[None], offset, rows, block_rows, key_block
        )
        low_parts.append(jnp.dot(part, frozen_down_factor, preferred_element_type=F32))
        halves, slots = gather_row(part[None], n_row)
        gathered.append(halves)
    order = jnp.bitwise_xor(row, jnp.array(slots, jnp.int32))

    coords = tile_placement.reshape(-1, 2)
    coords, bounds = tie(coords, bounds)
    tile_in, tile_out = coords[:, 0], coords[:, 1]
    weight = add_tiles(output_projection_weight, correction_tiles.reshape(-1, TILE, TILE), tile_in, tile_out)
    tile_slot = jnp.mod(tile_out // seg_tiles - col, n_col)
    tile_out = tile_out % seg_tiles

    inverse = jnp.array([slots.index(s) for s in range(n_row)], jnp.int32)
    batch_slot = inverse[jnp.bitwise_xor(row, jnp.arange(n_row))]

    jobs = []
    for q, (offset, rows) in enumerate(chunks):
        if rows == block_rows:
            jobs.append((q, 0, n_row, jnp.concatenate(gathered[q])))
        else:
            jobs.extend((q, h * half_rows, half_rows, gathered[q][h]) for h in range(2))
    jobs = [
        (q, lead, count, jnp.dot(part.reshape(count * chunks[q][1], width), weight, preferred_element_type=F32))
        for q, lead, count, part in jobs
    ]

    low_steps = low_rank_steps(jnp.concatenate(low_parts), col, n_col, n_row)
    low_next = next(low_steps)
    low_pending, low_done = None, None
    last = [{}, {}]
    got = [None] * len(jobs)
    streams = []
    for q, lead, count, _ in jobs:
        offset, rows = chunks[q]
        streams.append({way: [first_hop[way][lead:lead + count, offset:offset + rows]] for way in ways})
    for first in range(0, len(jobs), 2):
        for t in range(n_col - 1):
            for lane, at in enumerate(range(first, min(first + 2, len(jobs)))):
                q, lead, count, terms = jobs[at]
                sends = {}
                for way in ways:
                    send = lax.dynamic_slice_in_dim(terms, target(way, t, n_col) * segment, segment, 1)
                    if t > 0:
                        send = send + got[at][way].astype(F32)
                    send = send.astype(BF16)
                    if t + 1 < n_col - 1:
                        place = col if way > 0 else n_col - 1 - col
                        send = jnp.where(place <= t, send, streams[at][way][-1].reshape(send.shape))
                    sends[way] = send
                before = [last[lane][way] for way in ways] if last[lane] else []
                if low_pending is not None and lane == 1:
                    before = before + [low_pending]
                tied = tie(*[sends[way] for way in ways], *before)
                if low_pending is not None and lane == 1:
                    low_next = low_steps.send(tied[-1])
                    low_pending = None
                    if low_next[0] == "done":
                        low_done = low_next[1]
                        low_next = None
                arrived = {way: hop(tied[i], way, n_col, range(n_col)) for i, way in enumerate(ways)}
                if lane == 0 and low_next is not None and low_pending is None:
                    move, value = low_next
                    if before:
                        value, *_ = tie(value, *tied[len(ways):])
                    low_pending = move(value)
                last[lane] = arrived
                got[at] = arrived
                if t + 1 < n_col - 1:
                    for way in ways:
                        streams[at][way].append(
                            arrived[way].reshape(count, chunks[q][1], segment)
                        )
    while low_done is None:
        if low_pending is None:
            low_pending = low_next[0](low_next[1])
        low_next = low_steps.send(low_pending)
        low_pending = None
        if low_next[0] == "done":
            low_done = low_next[1]
    low = low_done
    low_ordered = low[batch_slot]

    up_here = lax.dynamic_slice_in_dim(trained_up_factor, col * segment, segment, 1)
    projected = jnp.zeros((n_row, local_len, segment), BF16)
    for at, (q, lead, count, terms) in enumerate(jobs):
        offset, rows = chunks[q]
        for j in range(count):
            low_term = jnp.dot(low[lead + j, offset:offset + rows], up_here, preferred_element_type=F32)
            mine = lax.dynamic_slice(terms, (j * rows, col * segment), (rows, segment))
            sums = mine + LOW_RANK_FACTOR * low_term
            for way in ways:
                sums = sums + got[at][way][j * rows:(j + 1) * rows].astype(F32)
            projected = lax.dynamic_update_slice(
                projected, sums.astype(BF16)[None], (order[lead + j], offset, 0)
            )

    tile_sum = jnp.zeros((coords.shape[0], TILE, TILE), F32)
    up_total = jnp.zeros((rank, out_width), F32)
    for q, (offset, rows) in enumerate(chunks):
        parts = []
        for at, job in enumerate(jobs):
            if job[0] == q:
                own = cotangent[job[1]:job[1] + job[2], offset:offset + rows]
                parts.append([own] + by_slot(streams[at][1], streams[at][-1], n_col))
        cot = jnp.concatenate(
            [jnp.concatenate([part[k] for part in parts])[None] for k in range(n_col)]
        )
        tile_sum = tile_sum + tile_grads(gathered[q], cot, tile_in, tile_slot, tile_out, order)
        up_total = up_grad(
            col,
            low_ordered[:, offset:offset + rows].reshape(n_row * rows, rank),
            cot.reshape(n_col, n_row * rows, segment),
            up_total,
        )

    up_gradient = add_over_seq(up_total, n_seq)
    tile_total = add_over_seq(tile_sum, n_seq)
    return projected, up_gradient, tile_total.reshape(correction_tiles.shape)


def solution(mesh):
    placed = (
        P("row", "seq", "col"),
        P("row", "seq", "col"),
        P("row", "seq", "col"),
        P("row", None),
        P("col", "row"),
        P("col", None),
        P(None, "row"),
        P("row", "col", None, None, None),
        P("row", "col", None, None),
        P(None, "seq", ("row", "col")),
    )
    return jax.shard_map(
        local,
        mesh=mesh,
        in_specs=placed,
        out_specs=(
            P(None, "seq", ("row", "col")),
            P(None, "row"),
            P("row", "col", None, None, None),
        ),
        check_vma=False,
    )
```

```python
import functools

import jax
import jax.numpy as jnp
from jax import lax
from jax.experimental import pallas as pl
from jax.experimental.pallas import tpu as pltpu
from jax.sharding import PartitionSpec as P

HEAD_WIDTH = 128
TILE = 128
F32 = jnp.float32
BF16 = jnp.bfloat16
LOW_RANK_FACTOR = 2.0
NEG = -1e30
LOG2E = 1.4426950408889634


def attend_kernel(bounds_ref, q_ref, k_ref, vt_ref, start_ref, o_ref, *, heads, key_block, first, blocks):
    rows = q_ref.shape[0]
    block = first + pl.program_id(2)
    scale = HEAD_WIDTH ** (-0.5) * LOG2E
    starts = start_ref[...]
    positions = bounds_ref[2 * blocks] + block * rows + lax.broadcasted_iota(jnp.int32, (1, rows), 1)
    queries = [q_ref[:, h * HEAD_WIDTH:(h + 1) * HEAD_WIDTH] for h in range(heads)]

    def step(at, carry):
        base = pl.multiple_of(at * key_block, key_block)
        keys = k_ref[pl.ds(base, key_block), :]
        values = vt_ref[:, pl.ds(base, key_block)]
        key_pos = base + lax.broadcasted_iota(jnp.int32, (key_block, rows), 0)
        visible = (key_pos >= starts) & (key_pos <= positions)
        out = []
        for h in range(heads):
            top, total, acc = carry[h]
            scores = lax.dot_general(
                keys, queries[h], (((1,), (1,)), ((), ())), preferred_element_type=F32
            )
            scores = jnp.where(visible, scores * scale, NEG)
            new_top = jnp.maximum(top, jnp.max(scores, axis=0, keepdims=True))
            probs = jnp.exp2(scores - new_top)
            fade = jnp.exp2(top - new_top)
            total = total * fade + jnp.sum(probs, axis=0, keepdims=True)
            acc = acc * fade + jnp.dot(values, probs.astype(BF16), preferred_element_type=F32)
            out.append((new_top, total, acc))
        return tuple(out)

    start = tuple(
        (
            jnp.full((1, rows), NEG, F32),
            jnp.zeros((1, rows), F32),
            jnp.zeros((HEAD_WIDTH, rows), F32),
        )
        for _ in range(heads)
    )
    done = lax.fori_loop(bounds_ref[block], bounds_ref[blocks + block], step, start)
    for h in range(heads):
        _, total, acc = done[h]
        o_ref[:, h * HEAD_WIDTH:(h + 1) * HEAD_WIDTH] = jnp.transpose(acc / total).astype(BF16)


def attend_chunk(queries, keys, values_t, bounds, starts, offset, rows, block_rows, key_block):
    length, width = queries.shape
    key_len = keys.shape[0]
    kv_heads = keys.shape[1] // HEAD_WIDTH
    group = width // HEAD_WIDTH // kv_heads
    heads = min(8, group)
    steps = group // heads
    first = offset // block_rows
    grid_spec = pltpu.PrefetchScalarGridSpec(
        num_scalar_prefetch=1,
        grid=(kv_heads, steps, rows // block_rows),
        in_specs=[
            pl.BlockSpec((block_rows, heads * HEAD_WIDTH), lambda g, s, i, b: (first + i, g * steps + s)),
            pl.BlockSpec((key_len, HEAD_WIDTH), lambda g, s, i, b: (0, g)),
            pl.BlockSpec((HEAD_WIDTH, key_len), lambda g, s, i, b: (g, 0)),
            pl.BlockSpec((1, block_rows), lambda g, s, i, b: (0, first + i)),
        ],
        out_specs=pl.BlockSpec((block_rows, heads * HEAD_WIDTH), lambda g, s, i, b: (i, g * steps + s)),
    )
    work = rows * key_len // 3 * width
    return pl.pallas_call(
        functools.partial(
            attend_kernel, heads=heads, key_block=key_block, first=first, blocks=length // block_rows
        ),
        out_shape=jax.ShapeDtypeStruct((rows, width), BF16),
        grid_spec=grid_spec,
        compiler_params=pltpu.CompilerParams(vmem_limit_bytes=32 * 1024 * 1024),
        cost_estimate=pl.CostEstimate(
            flops=8 * work, bytes_accessed=4 * rows * width, transcendentals=work // HEAD_WIDTH
        ),
        name="attention",
    )(bounds, queries, keys, values_t, starts)


def add_tiles_kernel(in_ref, out_tile_ref, w_ref, tiles_ref, o_ref):
    o_ref[...] = w_ref[...]
    for t in range(tiles_ref.shape[0]):

        @pl.when(in_ref[t] == pl.program_id(0))
        def _(t=t):
            at = pl.ds(pl.multiple_of(out_tile_ref[t] * TILE, TILE), TILE)
            o_ref[:, at] = (o_ref[:, at].astype(F32) + tiles_ref[t].astype(F32)).astype(BF16)


def add_tiles(weight, tiles, tile_in, tile_out):
    depth, out_width = weight.shape
    grid_spec = pltpu.PrefetchScalarGridSpec(
        num_scalar_prefetch=2,
        grid=(depth // TILE,),
        in_specs=[
            pl.BlockSpec((TILE, out_width), lambda i, ti, to: (i, 0)),
            pl.BlockSpec(tiles.shape, lambda i, ti, to: (0, 0, 0)),
        ],
        out_specs=pl.BlockSpec((TILE, out_width), lambda i, ti, to: (i, 0)),
    )
    return pl.pallas_call(
        add_tiles_kernel,
        out_shape=jax.ShapeDtypeStruct(weight.shape, BF16),
        grid_spec=grid_spec,
        cost_estimate=pl.CostEstimate(flops=0, bytes_accessed=4 * depth * out_width, transcendentals=0),
        name="add_tiles",
    )(tile_in, tile_out, weight, tiles)


def tile_grad_kernel(in_ref, slot_ref, out_tile_ref, order_ref, *refs):
    o_ref = refs[-1]
    count = (len(refs) - 1) // 2
    total = jnp.zeros(o_ref.shape[1:], F32)
    for j in range(count):
        total += lax.dot_general(
            refs[j][0], refs[count + j][0, 0], (((0,), (0,)), ((), ())), preferred_element_type=F32
        )
    o_ref[0] = total


def tile_grads(halves, cot, tile_in, tile_slot, tile_out, order):
    rows = cot.shape[2]
    tiles = tile_in.shape[0]
    arrays, a_specs, c_specs = [], [], []
    for half in halves:
        for b in range(half.shape[0]):
            j = len(arrays)
            arrays.append(half)
            a_specs.append(pl.BlockSpec((1, rows, TILE), lambda t, ti, ts, to, od, b=b: (b, 0, ti[t])))
            c_specs.append(
                pl.BlockSpec((1, 1, rows, TILE), lambda t, ti, ts, to, od, j=j: (ts[t], od[j], 0, to[t]))
            )
    batches = len(arrays)
    grid_spec = pltpu.PrefetchScalarGridSpec(
        num_scalar_prefetch=4,
        grid=(tiles,),
        in_specs=a_specs + c_specs,
        out_specs=pl.BlockSpec((1, TILE, TILE), lambda t, ti, ts, to, od: (t, 0, 0)),
    )
    return pl.pallas_call(
        tile_grad_kernel,
        out_shape=jax.ShapeDtypeStruct((tiles, TILE, TILE), F32),
        grid_spec=grid_spec,
        compiler_params=pltpu.CompilerParams(vmem_limit_bytes=16 * 1024 * 1024),
        cost_estimate=pl.CostEstimate(
            flops=2 * tiles * batches * rows * TILE * TILE,
            bytes_accessed=4 * tiles * batches * rows * TILE,
            transcendentals=0,
        ),
        name="tile_gradient",
    )(tile_in, tile_slot, tile_out, order, *arrays, *([cot] * batches))


def up_grad_kernel(col_ref, low_ref, cot_ref, sum_ref, o_ref):
    o_ref[...] = sum_ref[...] + LOW_RANK_FACTOR * lax.dot_general(
        low_ref[...], cot_ref[0], (((0,), (0,)), ((), ())), preferred_element_type=F32
    )


def up_grad(col, low, cot, total):
    slots, length, segment = cot.shape
    rank = low.shape[1]
    grid_spec = pltpu.PrefetchScalarGridSpec(
        num_scalar_prefetch=1,
        grid=(slots,),
        in_specs=[
            pl.BlockSpec((length, rank), lambda k, c: (0, 0)),
            pl.BlockSpec((1, length, segment), lambda k, c: (k, 0, 0)),
            pl.BlockSpec((rank, segment), lambda k, c: (0, lax.rem(k + c[0], slots))),
        ],
        out_specs=pl.BlockSpec((rank, segment), lambda k, c: (0, lax.rem(k + c[0], slots))),
    )
    return pl.pallas_call(
        up_grad_kernel,
        out_shape=jax.ShapeDtypeStruct(total.shape, F32),
        grid_spec=grid_spec,
        input_output_aliases={3: 0},
        compiler_params=pltpu.CompilerParams(vmem_limit_bytes=24 * 1024 * 1024),
        cost_estimate=pl.CostEstimate(
            flops=2 * slots * length * segment * rank,
            bytes_accessed=2 * slots * length * segment,
            transcendentals=0,
        ),
        name="up_gradient",
    )(col[None], low, cot, total)


def swap(value, axis, bit, size):
    return lax.ppermute(value, axis, [(i, i ^ bit) for i in range(size)])


def row_bits(size):
    bits = []
    bit = size // 2
    while bit >= 1:
        bits.append(bit)
        bit //= 2
    return bits


def row_slots(size):
    slots = [0]
    for bit in row_bits(size):
        slots = slots + [s ^ bit for s in slots]
    return slots


def add_over_seq(value, size):
    if size == 2:
        return value + swap(value, "seq", 1, size)
    return lax.psum(value, "seq")


def hop(value, way, size, senders):
    pairs = [(i, i + 1) for i in senders if i + 1 < size]
    if way < 0:
        pairs = [(size - 1 - a, size - 1 - b) for a, b in pairs]
    return lax.ppermute(value, "col", pairs)


def by_slot(from_left, from_right, size):
    me = lax.axis_index("col")
    return [
        jnp.where(me + k < size, from_right[k - 1], from_left[size - 1 - k]) for k in range(1, size)
    ]


def target(way, t, size):
    me = lax.axis_index("col")
    last = size - 1
    return jnp.clip(last - t + me if way > 0 else t + me - last, 0, last)


def tie(*values):
    return lax.optimization_barrier(values)


def local(
    queries,
    rotated_key_heads,
    value_head_states,
    document_index,
    output_projection_weight,
    frozen_down_factor,
    trained_up_factor,
    correction_tiles,
    tile_placement,
    cotangent,
):
    n_row, n_col, n_seq = lax.axis_size("row"), lax.axis_size("col"), lax.axis_size("seq")
    row, col, seq = lax.axis_index("row"), lax.axis_index("col"), lax.axis_index("seq")
    local_len, width = queries.shape[1], queries.shape[2]
    out_width = output_projection_weight.shape[1]
    segment = out_width // n_col
    seg_tiles = segment // TILE
    rank = frozen_down_factor.shape[1]
    block_rows = max(128, local_len // 4)
    chunks = [(at, block_rows) for at in range(0, local_len, block_rows)]
    ways = (1, -1)

    here = jnp.stack([rotated_key_heads[0], value_head_states[0]])
    if n_seq == 2:
        other = swap(here, "seq", 1, 2)
        both = jnp.concatenate([jnp.where(seq == 0, here, other), jnp.where(seq == 0, other, here)], axis=1)
    else:
        both = lax.all_gather(here, "seq", axis=1, tiled=True)
    keys, values_t = both[0], both[1].T
    key_block = min(256, keys.shape[0])
    documents = document_index[0]
    starts_all = jnp.searchsorted(documents, documents, side="left", method="compare_all").astype(jnp.int32)
    base = seq * local_len
    starts = lax.dynamic_slice_in_dim(starts_all, base, local_len, 0)
    block_at = jnp.arange(local_len // block_rows) * block_rows
    bounds = jnp.concatenate(
        [starts[block_at] // key_block, (base + block_at + block_rows - 1) // key_block + 1, base[None]]
    ).astype(jnp.int32)

    whole_hop = {way: hop(cotangent, way, n_col, range(n_col)) for way in ways}
    first_hop = [
        {way: whole_hop[way][:, offset:offset + rows] for way in ways} for offset, rows in chunks
    ]

    coords = tile_placement.reshape(-1, 2)
    coords, bounds = tie(coords, bounds)
    tile_in, tile_out = coords[:, 0], coords[:, 1]
    weight = add_tiles(output_projection_weight, correction_tiles.reshape(-1, TILE, TILE), tile_in, tile_out)
    weight, bounds = tie(weight, bounds)
    tile_slot = jnp.mod(tile_out // seg_tiles - col, n_col)
    tile_out = tile_out % seg_tiles

    slots = row_slots(n_row)
    order = jnp.bitwise_xor(row, jnp.array(slots, jnp.int32))
    inverse = jnp.array([slots.index(s) for s in range(n_row)], jnp.int32)
    batch_slot = inverse[jnp.bitwise_xor(row, jnp.arange(n_row))]

    low_parts, gathered, terms = [], [], []
    state = {"bounds": bounds}

    def hold(*values):
        state["bounds"] = tie(state["bounds"], *values)[0]

    def attend(q):
        offset, rows = chunks[q]
        part = attend_chunk(
            queries[0], keys, values_t, state["bounds"], starts[None], offset, rows, block_rows, key_block
        )
        part, state["bounds"] = tie(part, state["bounds"])
        low_parts.append(jnp.dot(part, frozen_down_factor, preferred_element_type=F32))
        return part

    def gather(parts):
        whole = jnp.stack(parts)[None]
        for bit in row_bits(n_row):
            moved = swap(whole, "row", bit, n_row)
            state.setdefault("moved", []).append(moved)
            whole = jnp.concatenate([whole, moved])
        gathered.extend(whole[:, i] for i in range(len(parts)))

    late_parts = []
    for q in range(len(chunks)):
        if q == 3:
            hold(state["moved"][0])
        part = attend(q)
        if q < 2:
            gather([part])
        else:
            late_parts.append(part)
    if late_parts:
        gather(late_parts)

    def project(q):
        terms.append(
            jnp.dot(gathered[q].reshape(n_row * chunks[q][1], width), weight, preferred_element_type=F32)
        )

    got = [None] * len(chunks)
    streams = [{way: [first_hop[q][way]] for way in ways} for q in range(len(chunks))]

    def launch(q, t, before):
        sends = []
        for way in ways:
            send = lax.dynamic_slice_in_dim(terms[q], target(way, t, n_col) * segment, segment, 1)
            if t > 0:
                send = send + got[q][way].astype(F32)
            send = send.astype(BF16)
            if t + 1 < n_col - 1:
                place = col if way > 0 else n_col - 1 - col
                send = jnp.where(place <= t, send, streams[q][way][-1].reshape(send.shape))
            sends.append(send)
        tied = tie(*sends, *before)
        got[q] = {way: hop(tied[i], way, n_col, range(n_col)) for i, way in enumerate(ways)}
        if t + 1 < n_col - 1:
            for way in ways:
                streams[q][way].append(got[q][way].reshape(n_row, chunks[q][1], segment))
        return tied[len(ways):]

    def cot_of(q):
        offset, rows = chunks[q]
        parts = [cotangent[:, offset:offset + rows]] + by_slot(streams[q][1], streams[q][-1], n_col)
        return jnp.concatenate([part[None] for part in parts])

    def add_up(q, cot, total):
        offset, rows = chunks[q]
        return up_grad(
            col,
            state["low_ordered"][:, offset:offset + rows].reshape(n_row * rows, rank),
            cot.reshape(n_col, n_row * rows, segment),
            total,
        )

    cots = {}
    early = len(chunks) // 2

    def side():
        current = jnp.concatenate(low_parts)
        for bit in row_bits(n_col):
            half = current.shape[0] // 2
            upper = jnp.bitwise_and(col, bit) != 0
            keep = jnp.where(upper, current[half:], current[:half])
            give = jnp.where(upper, current[:half], current[half:])
            arrived = yield (lambda v, bit=bit: swap(v, "col", bit, n_col)), give.astype(BF16), 3
            current = keep + arrived.astype(F32)
        current = current.astype(BF16)
        for bit in reversed(row_bits(n_col)):
            arrived = yield (lambda v, bit=bit: swap(v, "col", bit, n_col)), current, 2
            upper = jnp.bitwise_and(col, bit) != 0
            current = jnp.concatenate(
                [jnp.where(upper, arrived, current), jnp.where(upper, current, arrived)]
            )
        current = current[None]
        for bit in row_bits(n_row):
            arrived = yield (lambda v, bit=bit: swap(v, "row", bit, n_row)), current, 1
            current = jnp.concatenate([current, arrived])
        state["low"] = current
        state["low_ordered"] = current[batch_slot]
        while any(q not in cots for q in range(early)):
            yield None
        total = jnp.zeros((rank, out_width), F32)
        for q in range(early):
            total = add_up(q, cots[q], total)
        if n_seq == 2:
            total = lax.reduce_precision(total, exponent_bits=8, mantissa_bits=7)
            arrived = yield (lambda v: swap(v, "seq", 1, n_seq)), total.astype(BF16), 99
            state["up_early"] = total + arrived.astype(F32)
        else:
            state["up_early"] = lax.psum(total, "seq")

    lanes = [list(range(lane, len(chunks), 2)) for lane in range(2)]
    rounds = []
    for at in range(len(lanes[0])):
        for t in range(n_col - 1):
            for lane in range(2):
                if at < len(lanes[lane]):
                    rounds.append((lane, lanes[lane][at], t))
    last = [None, None]
    steps = side()
    pending, wait, over = None, 0, False
    tile_sum = jnp.zeros((coords.shape[0], TILE, TILE), F32)
    tile_due = []

    def advance(value):
        try:
            item = steps.send(value)
        except StopIteration:
            return None, 0, True
        if item is None:
            return None, 0, False
        return item[0](item[1]), item[2], False

    pending, _, over = advance(None)
    for at, (lane, q, t) in enumerate(rounds):
        if q == len(terms):
            project(q)
        before = [last[lane][way] for way in ways] if last[lane] else []
        if at == 5 and len(terms) < len(chunks):
            project(len(terms))
            before.append(terms[-1])
        take_side = pending is not None and wait <= 0
        if take_side:
            before.append(pending)
        if tile_due and tile_due[0][0] <= at:
            before.insert(0, tile_due.pop(0)[1])
        seen = list(launch(q, t, before))
        for c in range(len(chunks)):
            if c not in cots and all(len(streams[c][way]) == n_col - 1 for way in ways):
                cots[c] = cot_of(c)
                tile_sum = tile_sum + tile_grads([gathered[c]], cots[c], tile_in, tile_slot, tile_out, order)
                if at + 3 < len(rounds):
                    tile_due.append((at + 3, tile_sum))
        wait -= 1
        if take_side:
            pending, wait, over = advance(seen.pop())
            wait -= 1
        elif pending is None and not over:
            pending, wait, over = advance(None)
            wait -= 1
        last[lane] = got[q]
    while not over:
        pending, _, over = advance(pending)
    low = state["low"]

    up_here = lax.dynamic_slice_in_dim(trained_up_factor, col * segment, segment, 1)
    projected = jnp.zeros((n_row, local_len, segment), BF16)
    for q, (offset, rows) in enumerate(chunks):
        for j in range(n_row):
            low_term = jnp.dot(low[j, offset:offset + rows], up_here, preferred_element_type=F32)
            mine = lax.dynamic_slice(terms[q], (j * rows, col * segment), (rows, segment))
            sums = mine + LOW_RANK_FACTOR * low_term
            for way in ways:
                sums = sums + got[q][way][j * rows:(j + 1) * rows].astype(F32)
            projected = lax.dynamic_update_slice(projected, sums.astype(BF16)[None], (order[j], offset, 0))

    total = jnp.zeros((rank, out_width), F32)
    for q in range(early, len(chunks)):
        total = add_up(q, cots[q], total)
    if n_seq == 2:
        total = lax.reduce_precision(total, exponent_bits=8, mantissa_bits=7)
        total = total + swap(total.astype(BF16), "seq", 1, n_seq).astype(F32)
    else:
        total = lax.psum(total, "seq")
    up_gradient = state["up_early"] + total
    tile_total = add_over_seq(tile_sum, n_seq)
    return projected, up_gradient, tile_total.reshape(correction_tiles.shape)


def solution(mesh):
    placed = (
        P("row", "seq", "col"),
        P("row", "seq", "col"),
        P("row", "seq", "col"),
        P("row", None),
        P("col", "row"),
        P("col", None),
        P(None, "row"),
        P("row", "col", None, None, None),
        P("row", "col", None, None),
        P(None, "seq", ("row", "col")),
    )
    return jax.shard_map(
        local,
        mesh=mesh,
        in_specs=placed,
        out_specs=(
            P(None, "seq", ("row", "col")),
            P(None, "row"),
            P("row", "col", None, None, None),
        ),
        check_vma=False,
    )
```

```python
import functools

import jax
import jax.numpy as jnp
from jax import lax
from jax.experimental import pallas as pl
from jax.experimental.pallas import tpu as pltpu
from jax.sharding import PartitionSpec as P

HEAD_WIDTH = 128
TILE = 128
F32 = jnp.float32
BF16 = jnp.bfloat16
LOW_RANK_FACTOR = 2.0
NEG = -1e30
LOG2E = 1.4426950408889634


def attend_kernel(bounds_ref, q_ref, k_ref, vt_ref, start_ref, o_ref, *, heads, key_block, first, blocks):
    rows = q_ref.shape[0]
    block = first + pl.program_id(2)
    scale = HEAD_WIDTH ** (-0.5) * LOG2E
    starts = start_ref[...]
    positions = bounds_ref[2 * blocks] + block * rows + lax.broadcasted_iota(jnp.int32, (1, rows), 1)
    queries = [q_ref[:, h * HEAD_WIDTH:(h + 1) * HEAD_WIDTH] for h in range(heads)]

    def step(at, carry):
        base = pl.multiple_of(at * key_block, key_block)
        keys = k_ref[pl.ds(base, key_block), :]
        values = vt_ref[:, pl.ds(base, key_block)]
        key_pos = base + lax.broadcasted_iota(jnp.int32, (key_block, rows), 0)
        visible = (key_pos >= starts) & (key_pos <= positions)
        out = []
        for h in range(heads):
            top, total, acc = carry[h]
            scores = lax.dot_general(
                keys, queries[h], (((1,), (1,)), ((), ())), preferred_element_type=F32
            )
            scores = jnp.where(visible, scores * scale, NEG)
            new_top = jnp.maximum(top, jnp.max(scores, axis=0, keepdims=True))
            probs = jnp.exp2(scores - new_top)
            fade = jnp.exp2(top - new_top)
            total = total * fade + jnp.sum(probs, axis=0, keepdims=True)
            acc = acc * fade + jnp.dot(values, probs.astype(BF16), preferred_element_type=F32)
            out.append((new_top, total, acc))
        return tuple(out)

    start = tuple(
        (
            jnp.full((1, rows), NEG, F32),
            jnp.zeros((1, rows), F32),
            jnp.zeros((HEAD_WIDTH, rows), F32),
        )
        for _ in range(heads)
    )
    done = lax.fori_loop(bounds_ref[block], bounds_ref[blocks + block], step, start)
    for h in range(heads):
        _, total, acc = done[h]
        o_ref[:, h * HEAD_WIDTH:(h + 1) * HEAD_WIDTH] = jnp.transpose(acc / total).astype(BF16)


def attend_chunk(queries, keys, values_t, bounds, starts, offset, rows, block_rows, key_block):
    length, width = queries.shape
    key_len = keys.shape[0]
    kv_heads = keys.shape[1] // HEAD_WIDTH
    group = width // HEAD_WIDTH // kv_heads
    heads = min(8, group)
    steps = group // heads
    first = offset // block_rows
    grid_spec = pltpu.PrefetchScalarGridSpec(
        num_scalar_prefetch=1,
        grid=(kv_heads, steps, rows // block_rows),
        in_specs=[
            pl.BlockSpec((block_rows, heads * HEAD_WIDTH), lambda g, s, i, b: (first + i, g * steps + s)),
            pl.BlockSpec((key_len, HEAD_WIDTH), lambda g, s, i, b: (0, g)),
            pl.BlockSpec((HEAD_WIDTH, key_len), lambda g, s, i, b: (g, 0)),
            pl.BlockSpec((1, block_rows), lambda g, s, i, b: (0, first + i)),
        ],
        out_specs=pl.BlockSpec((block_rows, heads * HEAD_WIDTH), lambda g, s, i, b: (i, g * steps + s)),
    )
    work = rows * key_len // 3 * width
    return pl.pallas_call(
        functools.partial(
            attend_kernel, heads=heads, key_block=key_block, first=first, blocks=length // block_rows
        ),
        out_shape=jax.ShapeDtypeStruct((rows, width), BF16),
        grid_spec=grid_spec,
        compiler_params=pltpu.CompilerParams(vmem_limit_bytes=32 * 1024 * 1024),
        cost_estimate=pl.CostEstimate(
            flops=8 * work, bytes_accessed=4 * rows * width, transcendentals=work // HEAD_WIDTH
        ),
        name="attention",
    )(bounds, queries, keys, values_t, starts)


def add_tiles_kernel(in_ref, out_tile_ref, w_ref, tiles_ref, o_ref):
    o_ref[...] = w_ref[...]
    for t in range(tiles_ref.shape[0]):

        @pl.when(in_ref[t] == pl.program_id(0))
        def _(t=t):
            at = pl.ds(pl.multiple_of(out_tile_ref[t] * TILE, TILE), TILE)
            o_ref[:, at] = (o_ref[:, at].astype(F32) + tiles_ref[t].astype(F32)).astype(BF16)


def add_tiles(weight, tiles, tile_in, tile_out):
    depth, out_width = weight.shape
    grid_spec = pltpu.PrefetchScalarGridSpec(
        num_scalar_prefetch=2,
        grid=(depth // TILE,),
        in_specs=[
            pl.BlockSpec((TILE, out_width), lambda i, ti, to: (i, 0)),
            pl.BlockSpec(tiles.shape, lambda i, ti, to: (0, 0, 0)),
        ],
        out_specs=pl.BlockSpec((TILE, out_width), lambda i, ti, to: (i, 0)),
    )
    return pl.pallas_call(
        add_tiles_kernel,
        out_shape=jax.ShapeDtypeStruct(weight.shape, BF16),
        grid_spec=grid_spec,
        cost_estimate=pl.CostEstimate(flops=0, bytes_accessed=4 * depth * out_width, transcendentals=0),
        name="add_tiles",
    )(tile_in, tile_out, weight, tiles)


def tile_grad_kernel(in_ref, slot_ref, out_tile_ref, order_ref, *refs):
    o_ref = refs[-1]
    count = (len(refs) - 1) // 2
    total = jnp.zeros(o_ref.shape[1:], F32)
    for j in range(count):
        total += lax.dot_general(
            refs[j][0], refs[count + j][0, 0], (((0,), (0,)), ((), ())), preferred_element_type=F32
        )
    o_ref[0] = total


def tile_grads(halves, cot, tile_in, tile_slot, tile_out, order):
    rows = cot.shape[2]
    tiles = tile_in.shape[0]
    arrays, a_specs, c_specs = [], [], []
    for half in halves:
        for b in range(half.shape[0]):
            j = len(arrays)
            arrays.append(half)
            a_specs.append(pl.BlockSpec((1, rows, TILE), lambda t, ti, ts, to, od, b=b: (b, 0, ti[t])))
            c_specs.append(
                pl.BlockSpec((1, 1, rows, TILE), lambda t, ti, ts, to, od, j=j: (ts[t], od[j], 0, to[t]))
            )
    batches = len(arrays)
    grid_spec = pltpu.PrefetchScalarGridSpec(
        num_scalar_prefetch=4,
        grid=(tiles,),
        in_specs=a_specs + c_specs,
        out_specs=pl.BlockSpec((1, TILE, TILE), lambda t, ti, ts, to, od: (t, 0, 0)),
    )
    return pl.pallas_call(
        tile_grad_kernel,
        out_shape=jax.ShapeDtypeStruct((tiles, TILE, TILE), F32),
        grid_spec=grid_spec,
        compiler_params=pltpu.CompilerParams(vmem_limit_bytes=16 * 1024 * 1024),
        cost_estimate=pl.CostEstimate(
            flops=2 * tiles * batches * rows * TILE * TILE,
            bytes_accessed=4 * tiles * batches * rows * TILE,
            transcendentals=0,
        ),
        name="tile_gradient",
    )(tile_in, tile_slot, tile_out, order, *arrays, *([cot] * batches))


def up_grad_kernel(col_ref, low_ref, cot_ref, sum_ref, o_ref):
    o_ref[...] = sum_ref[...] + LOW_RANK_FACTOR * lax.dot_general(
        low_ref[...], cot_ref[0], (((0,), (0,)), ((), ())), preferred_element_type=F32
    )


def up_grad(col, low, cot, total):
    slots, length, segment = cot.shape
    rank = low.shape[1]
    grid_spec = pltpu.PrefetchScalarGridSpec(
        num_scalar_prefetch=1,
        grid=(slots,),
        in_specs=[
            pl.BlockSpec((length, rank), lambda k, c: (0, 0)),
            pl.BlockSpec((1, length, segment), lambda k, c: (k, 0, 0)),
            pl.BlockSpec((rank, segment), lambda k, c: (0, lax.rem(k + c[0], slots))),
        ],
        out_specs=pl.BlockSpec((rank, segment), lambda k, c: (0, lax.rem(k + c[0], slots))),
    )
    return pl.pallas_call(
        up_grad_kernel,
        out_shape=jax.ShapeDtypeStruct(total.shape, F32),
        grid_spec=grid_spec,
        input_output_aliases={3: 0},
        compiler_params=pltpu.CompilerParams(vmem_limit_bytes=24 * 1024 * 1024),
        cost_estimate=pl.CostEstimate(
            flops=2 * slots * length * segment * rank,
            bytes_accessed=2 * slots * length * segment,
            transcendentals=0,
        ),
        name="up_gradient",
    )(col[None], low, cot, total)


def swap(value, axis, bit, size):
    return lax.ppermute(value, axis, [(i, i ^ bit) for i in range(size)])


def row_bits(size):
    bits = []
    bit = size // 2
    while bit >= 1:
        bits.append(bit)
        bit //= 2
    return bits


def row_slots(size):
    slots = [0]
    for bit in row_bits(size):
        slots = slots + [s ^ bit for s in slots]
    return slots


def add_over_seq(value, size):
    if size == 2:
        return value + swap(value, "seq", 1, size)
    return lax.psum(value, "seq")


def hop(value, way, size, senders):
    pairs = [(i, i + 1) for i in senders if i + 1 < size]
    if way < 0:
        pairs = [(size - 1 - a, size - 1 - b) for a, b in pairs]
    return lax.ppermute(value, "col", pairs)


def by_slot(from_left, from_right, size):
    me = lax.axis_index("col")
    return [
        jnp.where(me + k < size, from_right[k - 1], from_left[size - 1 - k]) for k in range(1, size)
    ]


def target(way, t, size):
    me = lax.axis_index("col")
    last = size - 1
    return jnp.clip(last - t + me if way > 0 else t + me - last, 0, last)


def tie(*values):
    return lax.optimization_barrier(values)


def local(
    queries,
    rotated_key_heads,
    value_head_states,
    document_index,
    output_projection_weight,
    frozen_down_factor,
    trained_up_factor,
    correction_tiles,
    tile_placement,
    cotangent,
):
    n_row, n_col, n_seq = lax.axis_size("row"), lax.axis_size("col"), lax.axis_size("seq")
    row, col, seq = lax.axis_index("row"), lax.axis_index("col"), lax.axis_index("seq")
    local_len, width = queries.shape[1], queries.shape[2]
    out_width = output_projection_weight.shape[1]
    segment = out_width // n_col
    seg_tiles = segment // TILE
    rank = frozen_down_factor.shape[1]
    block_rows = max(128, local_len // 4)
    chunks = [(at, block_rows) for at in range(0, local_len, block_rows)]
    ways = (1, -1)

    here = jnp.stack([rotated_key_heads[0], value_head_states[0]])
    if n_seq == 2:
        other = swap(here, "seq", 1, 2)
        both = jnp.concatenate([jnp.where(seq == 0, here, other), jnp.where(seq == 0, other, here)], axis=1)
    else:
        both = lax.all_gather(here, "seq", axis=1, tiled=True)
    keys, values_t = both[0], both[1].T
    key_block = min(256, keys.shape[0])
    documents = document_index[0]
    starts_all = jnp.searchsorted(documents, documents, side="left", method="compare_all").astype(jnp.int32)
    base = seq * local_len
    starts = lax.dynamic_slice_in_dim(starts_all, base, local_len, 0)
    block_at = jnp.arange(local_len // block_rows) * block_rows
    bounds = jnp.concatenate(
        [starts[block_at] // key_block, (base + block_at + block_rows - 1) // key_block + 1, base[None]]
    ).astype(jnp.int32)

    whole_hop = {way: hop(cotangent, way, n_col, range(n_col)) for way in ways}
    first_hop = [
        {way: whole_hop[way][:, offset:offset + rows] for way in ways} for offset, rows in chunks
    ]

    coords = tile_placement.reshape(-1, 2)
    coords, bounds = tie(coords, bounds)
    tile_in, tile_out = coords[:, 0], coords[:, 1]
    weight = add_tiles(output_projection_weight, correction_tiles.reshape(-1, TILE, TILE), tile_in, tile_out)
    weight, bounds = tie(weight, bounds)
    tile_slot = jnp.mod(tile_out // seg_tiles - col, n_col)
    tile_out = tile_out % seg_tiles

    slots = row_slots(n_row)
    order = jnp.bitwise_xor(row, jnp.array(slots, jnp.int32))
    inverse = jnp.array([slots.index(s) for s in range(n_row)], jnp.int32)
    batch_slot = inverse[jnp.bitwise_xor(row, jnp.arange(n_row))]

    low_parts, gathered, terms = [], [], []
    state = {"bounds": bounds}

    def hold(*values):
        state["bounds"] = tie(state["bounds"], *values)[0]

    def attend(q):
        offset, rows = chunks[q]
        part = attend_chunk(
            queries[0], keys, values_t, state["bounds"], starts[None], offset, rows, block_rows, key_block
        )
        part, state["bounds"] = tie(part, state["bounds"])
        low_parts.append(jnp.dot(part, frozen_down_factor, preferred_element_type=F32))
        return part

    def gather(parts):
        whole = jnp.stack(parts)[None]
        for bit in row_bits(n_row):
            moved = swap(whole, "row", bit, n_row)
            state.setdefault("moved", []).append(moved)
            whole = jnp.concatenate([whole, moved])
        gathered.extend(whole[:, i] for i in range(len(parts)))

    late_parts = []
    for q in range(len(chunks)):
        if q == 3:
            hold(state["moved"][0])
        part = attend(q)
        if q < 2:
            gather([part])
        else:
            late_parts.append(part)
    if late_parts:
        gather(late_parts)

    def project(q):
        terms.append(
            jnp.dot(gathered[q].reshape(n_row * chunks[q][1], width), weight, preferred_element_type=F32)
        )

    got = [None] * len(chunks)
    streams = [{way: [first_hop[q][way]] for way in ways} for q in range(len(chunks))]

    def launch(q, t, before):
        sends = []
        for way in ways:
            send = lax.dynamic_slice_in_dim(terms[q], target(way, t, n_col) * segment, segment, 1)
            if t > 0:
                send = send + got[q][way].astype(F32)
            send = send.astype(BF16)
            if t + 1 < n_col - 1:
                place = col if way > 0 else n_col - 1 - col
                send = jnp.where(place <= t, send, streams[q][way][-1].reshape(send.shape))
            sends.append(send)
        tied = tie(*sends, *before)
        got[q] = {way: hop(tied[i], way, n_col, range(n_col)) for i, way in enumerate(ways)}
        if t + 1 < n_col - 1:
            for way in ways:
                streams[q][way].append(got[q][way].reshape(n_row, chunks[q][1], segment))
        return tied[len(ways):]

    def cot_of(q):
        offset, rows = chunks[q]
        parts = [cotangent[:, offset:offset + rows]] + by_slot(streams[q][1], streams[q][-1], n_col)
        return jnp.concatenate([part[None] for part in parts])

    def add_up(q, cot, total):
        offset, rows = chunks[q]
        return up_grad(
            col,
            state["low_ordered"][:, offset:offset + rows].reshape(n_row * rows, rank),
            cot.reshape(n_col, n_row * rows, segment),
            total,
        )

    cots = {}
    early = len(chunks) // 2

    def side():
        current = jnp.concatenate(low_parts)
        for bit in row_bits(n_col):
            half = current.shape[0] // 2
            upper = jnp.bitwise_and(col, bit) != 0
            keep = jnp.where(upper, current[half:], current[:half])
            give = jnp.where(upper, current[:half], current[half:])
            arrived = yield (lambda v, bit=bit: swap(v, "col", bit, n_col)), give.astype(BF16), 3
            current = keep + arrived.astype(F32)
        current = current.astype(BF16)
        for bit in reversed(row_bits(n_col)):
            arrived = yield (lambda v, bit=bit: swap(v, "col", bit, n_col)), current, 2
            upper = jnp.bitwise_and(col, bit) != 0
            current = jnp.concatenate(
                [jnp.where(upper, arrived, current), jnp.where(upper, current, arrived)]
            )
        current = current[None]
        for bit in row_bits(n_row):
            arrived = yield (lambda v, bit=bit: swap(v, "row", bit, n_row)), current, 1
            current = jnp.concatenate([current, arrived])
        state["low"] = current
        state["low_ordered"] = current[batch_slot]
        while any(q not in cots for q in range(early)):
            yield None
        total = jnp.zeros((rank, out_width), F32)
        for q in range(early):
            total = add_up(q, cots[q], total)
        if n_seq == 2:
            total = lax.reduce_precision(total, exponent_bits=8, mantissa_bits=7)
            arrived = yield (lambda v: swap(v, "seq", 1, n_seq)), total.astype(BF16), 99
            state["up_early"] = total + arrived.astype(F32)
        else:
            state["up_early"] = lax.psum(total, "seq")

    lanes = [list(range(lane, len(chunks), 2)) for lane in range(2)]
    rounds = []
    for at in range(len(lanes[0])):
        for t in range(n_col - 1):
            for lane in range(2):
                if at < len(lanes[lane]):
                    rounds.append((lane, lanes[lane][at], t))
    last = [None, None]
    steps = side()
    pending, wait, over = None, 0, False
    tile_sum = jnp.zeros((coords.shape[0], TILE, TILE), F32)
    tile_due = []

    def advance(value):
        try:
            item = steps.send(value)
        except StopIteration:
            return None, 0, True
        if item is None:
            return None, 0, False
        return item[0](item[1]), item[2], False

    pending, _, over = advance(None)
    for at, (lane, q, t) in enumerate(rounds):
        if q == len(terms):
            project(q)
        before = [last[lane][way] for way in ways] if last[lane] else []
        if at == 5 and len(terms) < len(chunks):
            project(len(terms))
            before.append(terms[-1])
        take_side = pending is not None and (wait <= 0 or at == len(rounds) - 1)
        if take_side:
            before.append(pending)
        if tile_due and tile_due[0][0] <= at:
            before.insert(0, tile_due.pop(0)[1])
        ends = at == len(rounds) - 1 and "low" in state
        if ends:
            before += [state["low"], tile_in]
        seen = list(launch(q, t, before))
        if ends:
            tile_in = seen.pop()
            state["low"] = seen.pop()
        for c in range(len(chunks)):
            if c not in cots and all(len(streams[c][way]) == n_col - 1 for way in ways):
                cots[c] = cot_of(c)
                if c >= early:
                    continue
                tile_sum = tile_sum + tile_grads([gathered[c]], cots[c], tile_in, tile_slot, tile_out, order)
                if at + 3 < len(rounds) - 1:
                    tile_due.append((at + 3, tile_sum))
        wait -= 1
        if take_side:
            pending, wait, over = advance(seen.pop())
            wait -= 1
        elif pending is None and not over:
            pending, wait, over = advance(None)
            wait -= 1
        last[lane] = got[q]
    while not over:
        pending, _, over = advance(pending)
    low = state["low"]

    up_here = lax.dynamic_slice_in_dim(trained_up_factor, col * segment, segment, 1)
    projected = jnp.zeros((n_row, local_len, segment), BF16)
    for q, (offset, rows) in enumerate(chunks):
        for j in range(n_row):
            low_term = jnp.dot(low[j, offset:offset + rows], up_here, preferred_element_type=F32)
            mine = lax.dynamic_slice(terms[q], (j * rows, col * segment), (rows, segment))
            sums = mine + LOW_RANK_FACTOR * low_term
            for way in ways:
                sums = sums + got[q][way][j * rows:(j + 1) * rows].astype(F32)
            projected = lax.dynamic_update_slice(projected, sums.astype(BF16)[None], (order[j], offset, 0))

    total = jnp.zeros((rank, out_width), F32)
    for q in range(early, len(chunks)):
        total = add_up(q, cots[q], total)
        tile_sum = tile_sum + tile_grads([gathered[q]], cots[q], tile_in, tile_slot, tile_out, order)
    if n_seq == 2:
        flat = jnp.concatenate([total, tile_sum.reshape(-1, out_width)])
        flat = lax.reduce_precision(flat, exponent_bits=8, mantissa_bits=7)
        flat = flat + swap(flat.astype(BF16), "seq", 1, n_seq).astype(F32)
        total, tile_total = flat[:rank], flat[rank:].reshape(tile_sum.shape)
    else:
        total, tile_total = lax.psum((total, tile_sum), "seq")
    up_gradient = state["up_early"] + total
    return projected, up_gradient, tile_total.reshape(correction_tiles.shape)


def solution(mesh):
    placed = (
        P("row", "seq", "col"),
        P("row", "seq", "col"),
        P("row", "seq", "col"),
        P("row", None),
        P("col", "row"),
        P("col", None),
        P(None, "row"),
        P("row", "col", None, None, None),
        P("row", "col", None, None),
        P(None, "seq", ("row", "col")),
    )
    return jax.shard_map(
        local,
        mesh=mesh,
        in_specs=placed,
        out_specs=(
            P(None, "seq", ("row", "col")),
            P(None, "row"),
            P("row", "col", None, None, None),
        ),
        check_vma=False,
    )
```

```python
import functools

import jax
import jax.numpy as jnp
from jax import lax
from jax.experimental import pallas as pl
from jax.experimental.pallas import tpu as pltpu
from jax.sharding import PartitionSpec as P

HEAD_WIDTH = 128
TILE = 128
F32 = jnp.float32
BF16 = jnp.bfloat16
LOW_RANK_FACTOR = 2.0
NEG = -1e30
LOG2E = 1.4426950408889634


def attend_kernel(bounds_ref, q_ref, k_ref, vt_ref, start_ref, o_ref, *, heads, key_block, first, blocks):
    rows = q_ref.shape[0]
    block = first + pl.program_id(2)
    scale = HEAD_WIDTH ** (-0.5) * LOG2E
    starts = start_ref[...]
    positions = bounds_ref[2 * blocks] + block * rows + lax.broadcasted_iota(jnp.int32, (1, rows), 1)
    queries = [q_ref[:, h * HEAD_WIDTH:(h + 1) * HEAD_WIDTH] for h in range(heads)]

    def step(at, carry):
        base = pl.multiple_of(at * key_block, key_block)
        keys = k_ref[pl.ds(base, key_block), :]
        values = vt_ref[:, pl.ds(base, key_block)]
        key_pos = base + lax.broadcasted_iota(jnp.int32, (key_block, rows), 0)
        visible = (key_pos >= starts) & (key_pos <= positions)
        out = []
        for h in range(heads):
            top, total, acc = carry[h]
            scores = lax.dot_general(
                keys, queries[h], (((1,), (1,)), ((), ())), preferred_element_type=F32
            )
            scores = jnp.where(visible, scores * scale, NEG)
            new_top = jnp.maximum(top, jnp.max(scores, axis=0, keepdims=True))
            probs = jnp.exp2(scores - new_top)
            fade = jnp.exp2(top - new_top)
            total = total * fade + jnp.sum(probs, axis=0, keepdims=True)
            acc = acc * fade + jnp.dot(values, probs.astype(BF16), preferred_element_type=F32)
            out.append((new_top, total, acc))
        return tuple(out)

    start = tuple(
        (
            jnp.full((1, rows), NEG, F32),
            jnp.zeros((1, rows), F32),
            jnp.zeros((HEAD_WIDTH, rows), F32),
        )
        for _ in range(heads)
    )
    done = lax.fori_loop(bounds_ref[block], bounds_ref[blocks + block], step, start)
    for h in range(heads):
        _, total, acc = done[h]
        o_ref[:, h * HEAD_WIDTH:(h + 1) * HEAD_WIDTH] = jnp.transpose(acc / total).astype(BF16)


def attend_chunk(queries, keys, values_t, bounds, starts, offset, rows, block_rows, key_block):
    length, width = queries.shape
    key_len = keys.shape[0]
    kv_heads = keys.shape[1] // HEAD_WIDTH
    group = width // HEAD_WIDTH // kv_heads
    heads = min(8, group)
    steps = group // heads
    first = offset // block_rows
    grid_spec = pltpu.PrefetchScalarGridSpec(
        num_scalar_prefetch=1,
        grid=(kv_heads, steps, rows // block_rows),
        in_specs=[
            pl.BlockSpec((block_rows, heads * HEAD_WIDTH), lambda g, s, i, b: (first + i, g * steps + s)),
            pl.BlockSpec((key_len, HEAD_WIDTH), lambda g, s, i, b: (0, g)),
            pl.BlockSpec((HEAD_WIDTH, key_len), lambda g, s, i, b: (g, 0)),
            pl.BlockSpec((1, block_rows), lambda g, s, i, b: (0, first + i)),
        ],
        out_specs=pl.BlockSpec((block_rows, heads * HEAD_WIDTH), lambda g, s, i, b: (i, g * steps + s)),
    )
    work = rows * key_len // 3 * width
    return pl.pallas_call(
        functools.partial(
            attend_kernel, heads=heads, key_block=key_block, first=first, blocks=length // block_rows
        ),
        out_shape=jax.ShapeDtypeStruct((rows, width), BF16),
        grid_spec=grid_spec,
        compiler_params=pltpu.CompilerParams(vmem_limit_bytes=32 * 1024 * 1024),
        cost_estimate=pl.CostEstimate(
            flops=8 * work, bytes_accessed=4 * rows * width, transcendentals=work // HEAD_WIDTH
        ),
        name="attention",
    )(bounds, queries, keys, values_t, starts)


def add_tiles_kernel(in_ref, out_tile_ref, w_ref, tiles_ref, o_ref):
    o_ref[...] = w_ref[...]
    for t in range(tiles_ref.shape[0]):

        @pl.when(in_ref[t] == pl.program_id(0))
        def _(t=t):
            at = pl.ds(pl.multiple_of(out_tile_ref[t] * TILE, TILE), TILE)
            o_ref[:, at] = (o_ref[:, at].astype(F32) + tiles_ref[t].astype(F32)).astype(BF16)


def add_tiles(weight, tiles, tile_in, tile_out):
    depth, out_width = weight.shape
    grid_spec = pltpu.PrefetchScalarGridSpec(
        num_scalar_prefetch=2,
        grid=(depth // TILE,),
        in_specs=[
            pl.BlockSpec((TILE, out_width), lambda i, ti, to: (i, 0)),
            pl.BlockSpec(tiles.shape, lambda i, ti, to: (0, 0, 0)),
        ],
        out_specs=pl.BlockSpec((TILE, out_width), lambda i, ti, to: (i, 0)),
    )
    return pl.pallas_call(
        add_tiles_kernel,
        out_shape=jax.ShapeDtypeStruct(weight.shape, BF16),
        grid_spec=grid_spec,
        cost_estimate=pl.CostEstimate(flops=0, bytes_accessed=4 * depth * out_width, transcendentals=0),
        name="add_tiles",
    )(tile_in, tile_out, weight, tiles)


def tile_grad_kernel(in_ref, slot_ref, out_tile_ref, order_ref, *refs):
    o_ref = refs[-1]
    count = (len(refs) - 1) // 2
    total = jnp.zeros(o_ref.shape[1:], F32)
    for j in range(count):
        total += lax.dot_general(
            refs[j][0], refs[count + j][0, 0], (((0,), (0,)), ((), ())), preferred_element_type=F32
        )
    o_ref[0] = total


def tile_grads(halves, cot, tile_in, tile_slot, tile_out, order):
    rows = cot.shape[2]
    tiles = tile_in.shape[0]
    arrays, a_specs, c_specs = [], [], []
    for half in halves:
        for b in range(half.shape[0]):
            j = len(arrays)
            arrays.append(half)
            a_specs.append(pl.BlockSpec((1, rows, TILE), lambda t, ti, ts, to, od, b=b: (b, 0, ti[t])))
            c_specs.append(
                pl.BlockSpec((1, 1, rows, TILE), lambda t, ti, ts, to, od, j=j: (ts[t], od[j], 0, to[t]))
            )
    batches = len(arrays)
    grid_spec = pltpu.PrefetchScalarGridSpec(
        num_scalar_prefetch=4,
        grid=(tiles,),
        in_specs=a_specs + c_specs,
        out_specs=pl.BlockSpec((1, TILE, TILE), lambda t, ti, ts, to, od: (t, 0, 0)),
    )
    return pl.pallas_call(
        tile_grad_kernel,
        out_shape=jax.ShapeDtypeStruct((tiles, TILE, TILE), F32),
        grid_spec=grid_spec,
        compiler_params=pltpu.CompilerParams(vmem_limit_bytes=16 * 1024 * 1024),
        cost_estimate=pl.CostEstimate(
            flops=2 * tiles * batches * rows * TILE * TILE,
            bytes_accessed=4 * tiles * batches * rows * TILE,
            transcendentals=0,
        ),
        name="tile_gradient",
    )(tile_in, tile_slot, tile_out, order, *arrays, *([cot] * batches))


def up_grad_kernel(col_ref, low_ref, cot_ref, sum_ref, o_ref):
    o_ref[...] = sum_ref[...] + LOW_RANK_FACTOR * lax.dot_general(
        low_ref[...], cot_ref[0], (((0,), (0,)), ((), ())), preferred_element_type=F32
    )


def up_grad(col, low, cot, total):
    slots, length, segment = cot.shape
    rank = low.shape[1]
    grid_spec = pltpu.PrefetchScalarGridSpec(
        num_scalar_prefetch=1,
        grid=(slots,),
        in_specs=[
            pl.BlockSpec((length, rank), lambda k, c: (0, 0)),
            pl.BlockSpec((1, length, segment), lambda k, c: (k, 0, 0)),
            pl.BlockSpec((rank, segment), lambda k, c: (0, lax.rem(k + c[0], slots))),
        ],
        out_specs=pl.BlockSpec((rank, segment), lambda k, c: (0, lax.rem(k + c[0], slots))),
    )
    return pl.pallas_call(
        up_grad_kernel,
        out_shape=jax.ShapeDtypeStruct(total.shape, F32),
        grid_spec=grid_spec,
        input_output_aliases={3: 0},
        compiler_params=pltpu.CompilerParams(vmem_limit_bytes=24 * 1024 * 1024),
        cost_estimate=pl.CostEstimate(
            flops=2 * slots * length * segment * rank,
            bytes_accessed=2 * slots * length * segment,
            transcendentals=0,
        ),
        name="up_gradient",
    )(col[None], low, cot, total)


def swap(value, axis, bit, size):
    return lax.ppermute(value, axis, [(i, i ^ bit) for i in range(size)])


def row_bits(size):
    bits = []
    bit = size // 2
    while bit >= 1:
        bits.append(bit)
        bit //= 2
    return bits


def row_slots(size):
    slots = [0]
    for bit in row_bits(size):
        slots = slots + [s ^ bit for s in slots]
    return slots


def add_over_seq(value, size):
    if size == 2:
        return value + swap(value, "seq", 1, size)
    return lax.psum(value, "seq")


def hop(value, way, size, senders):
    pairs = [(i, i + 1) for i in senders if i + 1 < size]
    if way < 0:
        pairs = [(size - 1 - a, size - 1 - b) for a, b in pairs]
    return lax.ppermute(value, "col", pairs)


def by_slot(from_left, from_right, size):
    me = lax.axis_index("col")
    return [
        jnp.where(me + k < size, from_right[k - 1], from_left[size - 1 - k]) for k in range(1, size)
    ]


def target(way, t, size):
    me = lax.axis_index("col")
    last = size - 1
    return jnp.clip(last - t + me if way > 0 else t + me - last, 0, last)


def tie(*values):
    return lax.optimization_barrier(values)


def local(
    queries,
    rotated_key_heads,
    value_head_states,
    document_index,
    output_projection_weight,
    frozen_down_factor,
    trained_up_factor,
    correction_tiles,
    tile_placement,
    cotangent,
):
    n_row, n_col, n_seq = lax.axis_size("row"), lax.axis_size("col"), lax.axis_size("seq")
    row, col, seq = lax.axis_index("row"), lax.axis_index("col"), lax.axis_index("seq")
    local_len, width = queries.shape[1], queries.shape[2]
    out_width = output_projection_weight.shape[1]
    segment = out_width // n_col
    seg_tiles = segment // TILE
    rank = frozen_down_factor.shape[1]
    block_rows = max(128, local_len // 4)
    chunks = [(at, block_rows) for at in range(0, local_len, block_rows)]
    ways = (1, -1)

    here = jnp.stack([rotated_key_heads[0], value_head_states[0]])
    if n_seq == 2:
        other = swap(here, "seq", 1, 2)
        both = jnp.concatenate([jnp.where(seq == 0, here, other), jnp.where(seq == 0, other, here)], axis=1)
    else:
        both = lax.all_gather(here, "seq", axis=1, tiled=True)
    keys, values_t = both[0], both[1].T
    key_block = min(256, keys.shape[0])
    documents = document_index[0]
    starts_all = jnp.searchsorted(documents, documents, side="left", method="compare_all").astype(jnp.int32)
    base = seq * local_len
    starts = lax.dynamic_slice_in_dim(starts_all, base, local_len, 0)
    block_at = jnp.arange(local_len // block_rows) * block_rows
    bounds = jnp.concatenate(
        [starts[block_at] // key_block, (base + block_at + block_rows - 1) // key_block + 1, base[None]]
    ).astype(jnp.int32)

    whole_hop = {way: hop(cotangent, way, n_col, range(n_col)) for way in ways}
    first_hop = [
        {way: whole_hop[way][:, offset:offset + rows] for way in ways} for offset, rows in chunks
    ]

    coords = tile_placement.reshape(-1, 2)
    coords, bounds = tie(coords, bounds)
    tile_in, tile_out = coords[:, 0], coords[:, 1]
    weight = add_tiles(output_projection_weight, correction_tiles.reshape(-1, TILE, TILE), tile_in, tile_out)
    weight, bounds = tie(weight, bounds)
    tile_slot = jnp.mod(tile_out // seg_tiles - col, n_col)
    tile_out = tile_out % seg_tiles

    slots = row_slots(n_row)
    order = jnp.bitwise_xor(row, jnp.array(slots, jnp.int32))
    inverse = jnp.array([slots.index(s) for s in range(n_row)], jnp.int32)
    batch_slot = inverse[jnp.bitwise_xor(row, jnp.arange(n_row))]

    low_parts, gathered, terms = [], [], []
    state = {"bounds": bounds}

    def hold(*values):
        state["bounds"] = tie(state["bounds"], *values)[0]

    def attend(q):
        offset, rows = chunks[q]
        part = attend_chunk(
            queries[0], keys, values_t, state["bounds"], starts[None], offset, rows, block_rows, key_block
        )
        part, state["bounds"] = tie(part, state["bounds"])
        low_parts.append(jnp.dot(part, frozen_down_factor, preferred_element_type=F32))
        return part

    def gather(parts):
        whole = jnp.stack(parts)[None]
        for bit in row_bits(n_row):
            moved = swap(whole, "row", bit, n_row)
            state.setdefault("moved", []).append(moved)
            whole = jnp.concatenate([whole, moved])
        gathered.extend(whole[:, i] for i in range(len(parts)))

    late_parts = []
    for q in range(len(chunks)):
        if q == 3:
            hold(state["moved"][0])
        part = attend(q)
        if q < 2:
            gather([part])
        else:
            late_parts.append(part)
    if late_parts:
        gather(late_parts)

    def project(q):
        terms.append(
            jnp.dot(gathered[q].reshape(n_row * chunks[q][1], width), weight, preferred_element_type=F32)
        )

    got = [None] * len(chunks)
    streams = [{way: [first_hop[q][way]] for way in ways} for q in range(len(chunks))]

    def launch(q, t, before):
        sends = []
        for way in ways:
            send = lax.dynamic_slice_in_dim(terms[q], target(way, t, n_col) * segment, segment, 1)
            if t > 0:
                send = send + got[q][way].astype(F32)
            send = send.astype(BF16)
            if t + 1 < n_col - 1:
                place = col if way > 0 else n_col - 1 - col
                send = jnp.where(place <= t, send, streams[q][way][-1].reshape(send.shape))
            sends.append(send)
        tied = tie(*sends, *before)
        got[q] = {way: hop(tied[i], way, n_col, range(n_col)) for i, way in enumerate(ways)}
        if t + 1 < n_col - 1:
            for way in ways:
                streams[q][way].append(got[q][way].reshape(n_row, chunks[q][1], segment))
        return tied[len(ways):]

    def cot_of(q):
        offset, rows = chunks[q]
        parts = [cotangent[:, offset:offset + rows]] + by_slot(streams[q][1], streams[q][-1], n_col)
        return jnp.concatenate([part[None] for part in parts])

    def add_up(q, cot, total):
        offset, rows = chunks[q]
        return up_grad(
            col,
            state["low_ordered"][:, offset:offset + rows].reshape(n_row * rows, rank),
            cot.reshape(n_col, n_row * rows, segment),
            total,
        )

    cots = {}
    early = len(chunks) // 2

    def side():
        current = jnp.concatenate(low_parts)
        for bit in row_bits(n_col):
            half = current.shape[0] // 2
            upper = jnp.bitwise_and(col, bit) != 0
            keep = jnp.where(upper, current[half:], current[:half])
            give = jnp.where(upper, current[:half], current[half:])
            arrived = yield (lambda v, bit=bit: swap(v, "col", bit, n_col)), give.astype(BF16), 3
            current = keep + arrived.astype(F32)
        current = current.astype(BF16)
        for bit in reversed(row_bits(n_col)):
            arrived = yield (lambda v, bit=bit: swap(v, "col", bit, n_col)), current, 2
            upper = jnp.bitwise_and(col, bit) != 0
            current = jnp.concatenate(
                [jnp.where(upper, arrived, current), jnp.where(upper, current, arrived)]
            )
        current = current[None]
        for bit in row_bits(n_row):
            arrived = yield (lambda v, bit=bit: swap(v, "row", bit, n_row)), current, 1
            current = jnp.concatenate([current, arrived])
        state["low"] = current
        state["low_ordered"] = current[batch_slot]
        while any(q not in cots for q in range(early)):
            yield None
        total = jnp.zeros((rank, out_width), F32)
        for q in range(early):
            total = add_up(q, cots[q], total)
        if n_seq == 2:
            total = lax.reduce_precision(total, exponent_bits=8, mantissa_bits=7)
            arrived = yield (lambda v: swap(v, "seq", 1, n_seq)), total.astype(BF16), 99
            state["up_early"] = total + arrived.astype(F32)
        else:
            state["up_early"] = lax.psum(total, "seq")

    lanes = [list(range(lane, len(chunks), 2)) for lane in range(2)]
    rounds = []
    for at in range(len(lanes[0])):
        for t in range(n_col - 1):
            for lane in range(2):
                if at < len(lanes[lane]):
                    rounds.append((lane, lanes[lane][at], t))
    last = [None, None]
    steps = side()
    pending, wait, over = None, 0, False
    tile_sum = jnp.zeros((coords.shape[0], TILE, TILE), F32)
    tile_due = []

    def advance(value):
        try:
            item = steps.send(value)
        except StopIteration:
            return None, 0, True
        if item is None:
            return None, 0, False
        return item[0](item[1]), item[2], False

    pending, _, over = advance(None)
    for at, (lane, q, t) in enumerate(rounds):
        if q == len(terms):
            project(q)
        before = [last[lane][way] for way in ways] if last[lane] else []
        if at == 5 and len(terms) < len(chunks):
            project(len(terms))
            before.append(terms[-1])
        take_side = pending is not None and (wait <= 0 or at == len(rounds) - 1)
        if take_side:
            before.append(pending)
        if tile_due and tile_due[0][0] <= at:
            before.insert(0, tile_due.pop(0)[1])
        ends = at == len(rounds) - 1 and "low" in state
        if ends:
            before += [state["low"], tile_in]
        seen = list(launch(q, t, before))
        if ends:
            tile_in = seen.pop()
            state["low"] = seen.pop()
        for c in range(len(chunks)):
            if c not in cots and all(len(streams[c][way]) == n_col - 1 for way in ways):
                cots[c] = cot_of(c)
                if c >= early:
                    continue
                tile_sum = tile_sum + tile_grads([gathered[c]], cots[c], tile_in, tile_slot, tile_out, order)
                if at + 5 < len(rounds) - 1:
                    tile_due.append((at + 5, tile_sum))
        wait -= 1
        if take_side:
            pending, wait, over = advance(seen.pop())
            wait -= 1
        elif pending is None and not over:
            pending, wait, over = advance(None)
            wait -= 1
        last[lane] = got[q]
    while not over:
        pending, _, over = advance(pending)
    low = state["low"]

    up_here = lax.dynamic_slice_in_dim(trained_up_factor, col * segment, segment, 1)
    projected = jnp.zeros((n_row, local_len, segment), BF16)
    for q, (offset, rows) in enumerate(chunks):
        for j in range(n_row):
            low_term = jnp.dot(low[j, offset:offset + rows], up_here, preferred_element_type=F32)
            mine = lax.dynamic_slice(terms[q], (j * rows, col * segment), (rows, segment))
            sums = mine + LOW_RANK_FACTOR * low_term
            for way in ways:
                sums = sums + got[q][way][j * rows:(j + 1) * rows].astype(F32)
            projected = lax.dynamic_update_slice(projected, sums.astype(BF16)[None], (order[j], offset, 0))

    total = jnp.zeros((rank, out_width), F32)
    for q in range(early, len(chunks)):
        total = add_up(q, cots[q], total)
        tile_sum = tile_sum + tile_grads([gathered[q]], cots[q], tile_in, tile_slot, tile_out, order)
    if n_seq == 2:
        flat = jnp.concatenate([total, tile_sum.reshape(-1, out_width)])
        flat = lax.reduce_precision(flat, exponent_bits=8, mantissa_bits=7)
        flat = flat + swap(flat.astype(BF16), "seq", 1, n_seq).astype(F32)
        total, tile_total = flat[:rank], flat[rank:].reshape(tile_sum.shape)
    else:
        total, tile_total = lax.psum((total, tile_sum), "seq")
    up_gradient = state["up_early"] + total
    return projected, up_gradient, tile_total.reshape(correction_tiles.shape)


def solution(mesh):
    placed = (
        P("row", "seq", "col"),
        P("row", "seq", "col"),
        P("row", "seq", "col"),
        P("row", None),
        P("col", "row"),
        P("col", None),
        P(None, "row"),
        P("row", "col", None, None, None),
        P("row", "col", None, None),
        P(None, "seq", ("row", "col")),
    )
    return jax.shard_map(
        local,
        mesh=mesh,
        in_specs=placed,
        out_specs=(
            P(None, "seq", ("row", "col")),
            P(None, "row"),
            P("row", "col", None, None, None),
        ),
        check_vma=False,
    )
```
